256 devices in a mesh: clip: 32 (over z, y_lo, core), seq: 8 (over x, y_hi).
Axes of the slice: x: 4, y: 4 (y_hi: 2, y_lo: 2; y = y_hi * 2 + y_lo), z: 8, core: 2. Of those that a mesh axis runs over, the one named last changes fastest.
Arguments:
- query_rows: bfloat16 [32, 1536, 5120], P('clip', 'seq'), may hold values from -32 to 32
- key_rows: bfloat16 [32, 1536, 5120], P('clip', 'seq'), may hold values from -32 to 32
- value_rows: bfloat16 [32, 1536, 5120], P('clip', 'seq'), may hold values from -6 to 6
- query_gain: float32 [5120], replicated, may hold values from 0.1 to 1.9
- key_gain: float32 [5120], replicated, may hold values from 0.1 to 1.9
- tile_lists: int32 [32, 40, 12, 12], P(None, 'seq'), may hold values from 0 to 11, as said below
- tile_counts: int32 [32, 40, 12], P(None, 'seq'), may hold values from 1 to 12, as said below
Outputs:
- attended: bfloat16 [32, 1536, 5120], P('clip', 'seq')
The draws below stay inside these ranges and needn't reach their ends.
Inputs may be any that keep to these rules, and one draw needn't show every extreme that they name: Each row tile_lists[c, h, b] is a permutation of 0 to 11 whose first entry is b; only its first tile_counts[c, h, b] entries are used. `tile_counts`: some entry equals 12 in every draw.
All inputs are finite; a program needn't handle non-finite values.
Results may differ from the reference program's by a relative error of at most 0.012.
The reference program's roundings to bfloat16 on the way count: a program that leaves them out, or rounds other values in their place, can miss the bound.
Values may be sent and summed in bfloat16 or wider, within the bound.
No kernel may reach another device: no remote copies, remote signals or barrier semaphores. Data moves between devices by JAX's collectives and lax.ppermute only.
A program may use at most 128 MiB of HBM per device.

```python
import math
import jax
import jax.numpy as jnp
from jax import lax

H = 40
HD = 128
D = 5120
BLK = 128
L = 1536
QB = 12
CLIPS = 32


def draw_query_rows(key, part):
    own_key = jax.random.fold_in(key, 7)
    return jnp.clip(jax.random.normal(own_key, (CLIPS, L, D), jnp.float32), -4.0, 4.0).astype(jnp.bfloat16)


def draw_key_rows(key, part):
    own_key = jax.random.fold_in(key, 9)
    return jnp.clip(jax.random.normal(own_key, (CLIPS, L, D), jnp.float32), -4.0, 4.0).astype(jnp.bfloat16)


def draw_tile_lists(key, part):
    key = jax.random.fold_in(key, 41)
    noise = jax.random.randint(key, (CLIPS, H, QB, QB), 0, 1 << 20, dtype=jnp.int32)
    blocks = jnp.arange(QB, dtype=jnp.int32)
    ordering = noise * QB + blocks
    ordering = jnp.where(blocks[:, None] == blocks[None, :], -1, ordering)
    return jnp.argsort(ordering, axis=-1, stable=True).astype(jnp.int32)


def draw_tile_counts(key, part):
    key = jax.random.fold_in(key, 31)
    level_key, count_key, spot_key = jax.random.split(key, 3)
    level = jax.random.randint(level_key, (CLIPS, 1, 1), 1, QB + 1, dtype=jnp.int32)
    counts = 1 + jax.random.randint(count_key, (CLIPS, H, QB), 0, level, dtype=jnp.int32)
    spot = jax.random.randint(spot_key, (3,), 0, jnp.array([CLIPS, H, QB], dtype=jnp.int32), dtype=jnp.int32)
    counts = counts.at[spot[0], spot[1], spot[2]].set(QB)
    return counts.astype(jnp.int32)


def block_levels(stream_key, extent, pieces, low, largest):
    level = 1.0
    for position, shards_of in pieces:
        draws = jax.random.uniform(jax.random.fold_in(jax.random.fold_in(stream_key, 6), position), (shards_of,), jnp.float32, low / len(pieces), largest / len(pieces))
        level = level * jnp.repeat(jnp.exp(draws), extent[position] // shards_of).reshape((-1,) + (1,) * (len(extent) - 1 - position))
    return level


def bell_draw(rng, dims, scale, most, shards=(), held_as=jnp.bfloat16):
    drawn = jax.random.normal(rng, dims, jnp.float32) * scale
    if len(shards) > 0:
        drawn = block_levels(rng, dims, shards, -0.22, 0.18) * drawn
    return jnp.clip(drawn, min=-most, max=most).astype(held_as)


def setup_inputs(seed: int = 0) -> dict:
    arg_keys = jax.random.split(jax.random.key(seed), 8)
    return {
        "query_rows": draw_query_rows(jax.random.fold_in(arg_keys[7], 71), 0),
        "key_rows": draw_key_rows(jax.random.fold_in(arg_keys[7], 71), 0),
        "value_rows": bell_draw(arg_keys[2], (CLIPS, L, D), 1.0, 6.0, ((0, 32), (1, 8))),
        "query_gain": jnp.clip(1.0 + 0.18 * jax.random.normal(arg_keys[3], (D,), jnp.float32), 0.1, 1.9),
        "key_gain": jnp.clip(1.0 + 0.18 * jax.random.normal(arg_keys[4], (D,), jnp.float32), 0.1, 1.9),
        "tile_lists": draw_tile_lists(jax.random.fold_in(arg_keys[7], 71), 0),
        "tile_counts": draw_tile_counts(jax.random.fold_in(arg_keys[7], 71), 0),
    }


epsilon = 1e-06

def rms_normed(rows, gain):
    values = rows.astype(jnp.float32)
    spread = lax.optimization_barrier(jnp.mean(values * values, axis=-1, keepdims=True))
    return (values * lax.rsqrt(spread + epsilon) * gain.astype(jnp.float32)).astype(jnp.bfloat16)

def block_allowed(tile_lists, tile_counts):
    blocks = jnp.arange(QB, dtype=jnp.int32)
    named_block = tile_lists[..., None] == blocks
    live_slot = blocks[:, None] < tile_counts[..., None, None]
    return jnp.any(named_block & live_slot, axis=-2)

def one_head(operands):
    query_head, key_head, value_head, allowed = operands
    scores = jnp.dot(query_head, key_head.T, preferred_element_type=jnp.float32)
    scores = scores * (1.0 / math.sqrt(HD))
    tile_mask = jnp.repeat(jnp.repeat(allowed, BLK, axis=0), BLK, axis=1)
    scores = jnp.where(tile_mask, scores, -jnp.inf)
    highest = lax.optimization_barrier(jnp.max(scores, axis=-1, keepdims=True))
    weights = jnp.exp(scores - highest)
    denominator = lax.optimization_barrier(jnp.sum(weights, axis=-1, keepdims=True))
    numerator = jnp.dot(weights.astype(jnp.bfloat16), value_head, preferred_element_type=jnp.float32)
    return (numerator / denominator).astype(jnp.bfloat16)

def heads_first(matrix):
    return matrix.reshape(L, H, HD).transpose(1, 0, 2)

def one_clip(operands):
    query_clip, key_clip, value_clip, allowed = operands
    outputs = lax.map(one_head, (heads_first(query_clip), heads_first(key_clip), heads_first(value_clip), allowed))
    return outputs.transpose(1, 0, 2).reshape(L, H * HD)

def reference(query_rows, key_rows, value_rows, query_gain, key_gain, tile_lists, tile_counts):
    query_normed = rms_normed(query_rows, query_gain)
    key_normed = rms_normed(key_rows, key_gain)
    allowed = block_allowed(tile_lists, tile_counts)
    return lax.map(one_clip, (query_normed, key_normed, value_rows, allowed))
```

```python
import math

import jax
import jax.numpy as jnp
from jax import lax
from jax.experimental import pallas as pl
from jax.experimental.pallas import tpu as pltpu
from jax.sharding import PartitionSpec as P

HD = 128
BLK = 128
EPSILON = 1e-06
CHUNKS = ((0, 2), (2, 5))
MIB = 1 << 20


def normed(rows, gain):
    values = rows.astype(jnp.float32)
    spread = jnp.mean(values * values, axis=-1, keepdims=True)
    return (values * lax.rsqrt(spread + EPSILON) * gain).astype(jnp.bfloat16)


def pack_heads(query_rows, key_rows, value_rows, query_gain, key_gain, parts, first, last):
    rows, width = query_rows.shape
    own = width // parts
    span = (last - first) * HD
    step = 32

    def kernel(q_ref, k_ref, v_ref, qg_ref, kg_ref, out_ref):
        q = normed(q_ref[...], qg_ref[...])
        k = normed(k_ref[...], kg_ref[...])
        for part in range(parts):
            cols = slice(part * own + first * HD, part * own + last * HD)
            out_ref[part, :, :span] = q[:, cols]
            out_ref[part, :, span : 2 * span] = k[:, cols]
            out_ref[part, :, 2 * span :] = v_ref[:, cols]

    row_spec = pl.BlockSpec((step, width), lambda i: (i, 0))
    gain_spec = pl.BlockSpec((1, width), lambda i: (0, 0))
    return pl.pallas_call(
        kernel,
        grid=(rows // step,),
        in_specs=[row_spec, row_spec, row_spec, gain_spec, gain_spec],
        out_specs=pl.BlockSpec((parts, step, 3 * span), lambda i: (0, i, 0)),
        out_shape=jax.ShapeDtypeStruct((parts, rows, 3 * span), jnp.bfloat16),
        compiler_params=pltpu.CompilerParams(vmem_limit_bytes=56 * MIB),
        cost_estimate=pl.CostEstimate(flops=12 * rows * width, bytes_accessed=12 * rows * width, transcendentals=0),
        name=f"pack_{first}",
    )(query_rows, key_rows, value_rows, query_gain, key_gain)


def attend(packed, bias):
    length = packed.shape[0]
    heads, blocks, _ = bias.shape
    factor = math.log2(math.e) / math.sqrt(HD)

    def kernel(q_ref, k_ref, v_ref, bias_ref, out_ref):
        def block(b, carry):
            rows = pl.ds(pl.multiple_of(b * BLK, BLK), BLK)
            scores = lax.dot_general(
                q_ref[rows, :], k_ref[...], (((1,), (1,)), ((), ())), preferred_element_type=jnp.float32
            )
            scores = scores + bias_ref[0, pl.ds(b, 1), :]
            top = jnp.max(scores, axis=-1, keepdims=True)
            weights = jnp.exp2((scores - top) * factor)
            total = jnp.sum(weights, axis=-1, keepdims=True)
            mixed = jnp.dot(weights.astype(jnp.bfloat16), v_ref[...], preferred_element_type=jnp.float32)
            out_ref[rows, :] = (mixed / total).astype(jnp.bfloat16)
            return carry

        lax.fori_loop(0, blocks, block, 0)

    return pl.pallas_call(
        kernel,
        grid=(heads,),
        in_specs=[
            pl.BlockSpec((length, HD), lambda h: (0, h)),
            pl.BlockSpec((length, HD), lambda h: (0, heads + h)),
            pl.BlockSpec((length, HD), lambda h: (0, 2 * heads + h)),
            pl.BlockSpec((1, blocks, length), lambda h: (h, 0, 0)),
        ],
        out_specs=pl.BlockSpec((length, HD), lambda h: (0, h)),
        out_shape=jax.ShapeDtypeStruct((length, heads * HD), jnp.bfloat16),
        compiler_params=pltpu.CompilerParams(vmem_limit_bytes=56 * MIB),
        cost_estimate=pl.CostEstimate(
            flops=4 * heads * length * length * HD,
            bytes_accessed=8 * heads * length * HD,
            transcendentals=heads * length * length,
        ),
        name=f"attend_{heads}",
    )(packed, packed, packed, bias)


def unpack_heads(pieces):
    parts, rows, _ = pieces[0].shape
    spans = [piece.shape[2] for piece in pieces]
    own = sum(spans)

    def kernel(*refs):
        out_ref = refs[-1]
        at = 0
        for ref, span in zip(refs[:-1], spans):
            out_ref[:, at : at + span] = ref[0]
            at += span

    return pl.pallas_call(
        kernel,
        grid=(parts,),
        in_specs=[pl.BlockSpec((1, rows, span), lambda i: (i, 0, 0)) for span in spans],
        out_specs=pl.BlockSpec((rows, own), lambda i: (0, i)),
        out_shape=jax.ShapeDtypeStruct((rows, parts * own), jnp.bfloat16),
        compiler_params=pltpu.CompilerParams(vmem_limit_bytes=56 * MIB),
        cost_estimate=pl.CostEstimate(flops=0, bytes_accessed=4 * rows * parts * own, transcendentals=0),
        name="unpack",
    )(*pieces)


def swap(blocks):
    return lax.all_to_all(blocks, "seq", 0, 0, tiled=True)


def shards(query_rows, key_rows, value_rows, query_gain, key_gain, tile_lists, tile_counts):
    parts = lax.axis_size("seq")
    _, rows, width = query_rows.shape
    length = rows * parts
    blocks = length // BLK
    heads = tile_lists.shape[1]
    args = (query_rows[0], key_rows[0], value_rows[0], query_gain[None], key_gain[None])
    arrived = []
    for first, last in CHUNKS:
        packed = pack_heads(*args, parts, first, last)
        packed, args, tile_lists, tile_counts = lax.optimization_barrier((packed, args, tile_lists, tile_counts))
        arrived.append(swap(packed))
    clip_index = lax.axis_index("clip")
    lists = lax.dynamic_index_in_dim(tile_lists, clip_index, 0, keepdims=False)
    counts = lax.dynamic_index_in_dim(tile_counts, clip_index, 0, keepdims=False)
    live = jnp.arange(blocks, dtype=jnp.int32) < counts[..., None]
    named = lists[..., None] == (jnp.arange(length, dtype=jnp.int32) // BLK)
    bias = jnp.where(jnp.any(named & live[..., None], axis=2), 0.0, -1e30).astype(jnp.float32)
    sent = []
    for packed, (first, last) in zip(arrived, CHUNKS):
        mixed = attend(packed.reshape(length, packed.shape[2]), bias[first:last])
        sent.append(swap(mixed.reshape(parts, rows, mixed.shape[1])))
    return unpack_heads(sent)[None]


def solution(mesh):
    in_specs = (
        P("clip", "seq", None),
        P("clip", "seq", None),
        P("clip", "seq", None),
        P(),
        P(),
        P(None, "seq", None, None),
        P(None, "seq", None),
    )
    out_specs = P("clip", "seq", None)
    return jax.shard_map(shards, mesh=mesh, in_specs=in_specs, out_specs=out_specs, check_vma=False)
```

```python
import math

import jax
import jax.numpy as jnp
from jax import lax
from jax.experimental import pallas as pl
from jax.experimental.pallas import tpu as pltpu
from jax.sharding import PartitionSpec as P

HD = 128
BLK = 128
EPSILON = 1e-06
SPLIT = 4
ORDER = ((1, 0), (3, 1), (3, 0), (1, 1), (0, 1), (2, 0), (2, 1))
WINDOW = 5
EARLY = 4
MIB = 1 << 20


def pack_heads(query_rows, key_rows, value_rows, query_gain, key_gain, parts, first, last):
    rows, width = query_rows.shape
    own = width // parts
    span = (last - first) * HD
    step = rows // 2

    def kernel(q_ref, k_ref, v_ref, qg_ref, kg_ref, out_ref):
        def inverse(ref):
            values = ref[...].astype(jnp.float32)
            return lax.rsqrt(jnp.mean(values * values, axis=-1, keepdims=True) + EPSILON)

        def scaled(ref, factor, gain_ref, cols):
            return (ref[:, cols].astype(jnp.float32) * factor * gain_ref[:, cols]).astype(jnp.bfloat16)

        q_factor = inverse(q_ref)
        k_factor = inverse(k_ref)
        for part in range(parts):
            cols = slice(part * own + first * HD, part * own + last * HD)
            out_ref[part, :, :span] = scaled(q_ref, q_factor, qg_ref, cols)
            out_ref[part, :, span : 2 * span] = scaled(k_ref, k_factor, kg_ref, cols)
            out_ref[part, :, 2 * span :] = v_ref[:, cols]

    row_spec = pl.BlockSpec((step, width), lambda i: (i, 0))
    gain_spec = pl.BlockSpec((1, width), lambda i: (0, 0))
    return pl.pallas_call(
        kernel,
        grid=(rows // step,),
        in_specs=[row_spec, row_spec, row_spec, gain_spec, gain_spec],
        out_specs=pl.BlockSpec((parts, step, 3 * span), lambda i: (0, i, 0)),
        out_shape=jax.ShapeDtypeStruct((parts, rows, 3 * span), jnp.bfloat16),
        compiler_params=pltpu.CompilerParams(vmem_limit_bytes=60 * MIB),
        cost_estimate=pl.CostEstimate(flops=12 * rows * width, bytes_accessed=12 * rows * width, transcendentals=0),
        name=f"pack_{first}",
    )(query_rows, key_rows, value_rows, query_gain, key_gain)


def pack_pieces(query_rows, key_rows, value_rows, query_gain, key_gain, targets, first, last):
    rows, width = query_rows.shape
    parts = targets.shape[0]
    own = width // parts
    span = (last - first) * HD
    step = rows // 2

    def kernel(target_ref, q_ref, k_ref, v_ref, qg_ref, kg_ref, *out_refs):
        def inverse(ref):
            values = ref[...].astype(jnp.float32)
            return lax.rsqrt(jnp.mean(values * values, axis=-1, keepdims=True) + EPSILON)

        def scaled(ref, factor, gain_ref, cols):
            return (ref[:, cols].astype(jnp.float32) * factor * gain_ref[:, cols]).astype(jnp.bfloat16)

        q_factor = inverse(q_ref)
        k_factor = inverse(k_ref)
        for o, out_ref in enumerate(out_refs):
            cols = pl.ds(pl.multiple_of(target_ref[o] * own + first * HD, HD), span)
            out_ref[:, :span] = scaled(q_ref, q_factor, qg_ref, cols)
            out_ref[:, span : 2 * span] = scaled(k_ref, k_factor, kg_ref, cols)
            out_ref[:, 2 * span :] = v_ref[:, cols]

    row_spec = pl.BlockSpec((step, width), lambda i, t: (i, 0))
    gain_spec = pl.BlockSpec((1, width), lambda i, t: (0, 0))
    return pl.pallas_call(
        kernel,
        grid_spec=pltpu.PrefetchScalarGridSpec(
            num_scalar_prefetch=1,
            grid=(rows // step,),
            in_specs=[row_spec, row_spec, row_spec, gain_spec, gain_spec],
            out_specs=[pl.BlockSpec((step, 3 * span), lambda i, t: (i, 0))] * parts,
        ),
        out_shape=[jax.ShapeDtypeStruct((rows, 3 * span), jnp.bfloat16)] * parts,
        compiler_params=pltpu.CompilerParams(vmem_limit_bytes=60 * MIB),
        cost_estimate=pl.CostEstimate(flops=12 * rows * width, bytes_accessed=12 * rows * width, transcendentals=0),
        name=f"pack_pieces_{first}",
    )(targets, query_rows, key_rows, value_rows, query_gain, key_gain)


def one_head(q_ref, k_ref, v_ref, bias_ref, out_ref):
    length = q_ref.shape[0]
    factor = math.log2(math.e) / math.sqrt(HD)

    def scored(i):
        raw = lax.dot_general(
            q_ref[i * BLK : (i + 1) * BLK, :],
            k_ref[...],
            (((1,), (1,)), ((), ())),
            preferred_element_type=jnp.float32,
        )
        return raw + bias_ref[i : i + 1, :]

    def finish(i, scores):
        top = jnp.max(scores, axis=-1, keepdims=True)
        weights = jnp.exp2((scores - top) * factor)
        total = jnp.sum(weights, axis=-1, keepdims=True)
        mixed = jnp.dot(weights.astype(jnp.bfloat16), v_ref[...], preferred_element_type=jnp.float32)
        out_ref[i * BLK : (i + 1) * BLK, :] = (mixed / total).astype(jnp.bfloat16)

    scores = scored(0)
    for i in range(length // BLK):
        ahead = scored(i + 1) if (i + 1) * BLK < length else None
        finish(i, scores)
        scores = ahead


def attend_pieces(pieces, bias, sources, first):
    parts = len(pieces)
    rows, width = pieces[0].shape
    heads = width // (3 * HD)
    all_heads, blocks, length = bias.shape

    def kernel(source_ref, bias_ref, *refs):
        in_refs = refs[:parts]
        out_ref, held, done, in_sems, out_sems = refs[parts:]

        def arrival(o, h, j):
            at = pl.multiple_of(source_ref[o] * rows, 64)
            cols = pl.ds((j * heads + h) * HD, HD)
            return pltpu.make_async_copy(in_refs[o].at[:, cols], held.at[pl.ds(at, rows), cols], in_sems.at[h, j, o])

        def departure(h):
            return pltpu.make_async_copy(
                done.at[:, pl.ds(h * HD, HD)], out_ref.at[:, pl.ds((first + h) * HD, HD)], out_sems.at[h]
            )

        for h in range(heads):
            for j in range(3):
                for o in range(parts):
                    arrival(o, h, j).start()
        for h in range(heads):
            for j in range(3):
                for o in range(parts):
                    arrival(o, h, j).wait()
            q, k, v = (held.at[:, (j * heads + h) * HD : (j * heads + h + 1) * HD] for j in range(3))
            one_head(q, k, v, bias_ref.at[first + h], done.at[:, h * HD : (h + 1) * HD])
            departure(h).start()
        for h in range(heads):
            departure(h).wait()

    anywhere = pl.BlockSpec(memory_space=pl.ANY)
    return pl.pallas_call(
        kernel,
        in_specs=[pl.BlockSpec(memory_space=pltpu.SMEM), pl.BlockSpec(memory_space=pltpu.VMEM)]
        + [anywhere] * parts,
        out_specs=anywhere,
        out_shape=jax.ShapeDtypeStruct((length, all_heads * HD), jnp.bfloat16),
        scratch_shapes=[
            pltpu.VMEM((length, width), jnp.bfloat16),
            pltpu.VMEM((length, heads * HD), jnp.bfloat16),
            pltpu.SemaphoreType.DMA((heads, 3, parts)),
            pltpu.SemaphoreType.DMA((heads,)),
        ],
        compiler_params=pltpu.CompilerParams(vmem_limit_bytes=60 * MIB),
        cost_estimate=pl.CostEstimate(
            flops=4 * heads * length * length * HD,
            bytes_accessed=8 * heads * length * HD,
            transcendentals=heads * length * length,
        ),
        name=f"attend_{heads}",
    )(sources, bias, *pieces)


def attend_blocks(packed, bias, first, mixed):
    length, width = packed.shape
    heads = width // (3 * HD)
    blocks = bias.shape[1]

    def kernel(q_ref, k_ref, v_ref, bias_ref, mixed_ref, out_ref):
        one_head(q_ref, k_ref, v_ref, bias_ref.at[0], out_ref)

    return pl.pallas_call(
        kernel,
        grid=(heads,),
        in_specs=[
            pl.BlockSpec((length, HD), lambda h: (0, h)),
            pl.BlockSpec((length, HD), lambda h: (0, heads + h)),
            pl.BlockSpec((length, HD), lambda h: (0, 2 * heads + h)),
            pl.BlockSpec((1, blocks, length), lambda h: (first + h, 0, 0)),
            pl.BlockSpec(memory_space=pl.ANY),
        ],
        out_specs=pl.BlockSpec((length, HD), lambda h: (0, first + h)),
        out_shape=jax.ShapeDtypeStruct(mixed.shape, mixed.dtype),
        input_output_aliases={4: 0},
        compiler_params=pltpu.CompilerParams(vmem_limit_bytes=60 * MIB),
        cost_estimate=pl.CostEstimate(
            flops=4 * heads * length * length * HD,
            bytes_accessed=8 * heads * length * HD,
            transcendentals=heads * length * length,
        ),
        name="attend_blocks",
    )(packed, packed, packed, bias, mixed)


def unpack_heads(pieces):
    parts, rows, _ = pieces[0].shape
    spans = [piece.shape[2] for piece in pieces]
    own = sum(spans)
    step = parts // 2

    def kernel(*refs):
        out_ref = refs[-1]
        at = 0
        for i in range(step):
            for ref, span in zip(refs[:-1], spans):
                out_ref[:, at : at + span] = ref[i]
                at += span

    return pl.pallas_call(
        kernel,
        grid=(parts // step,),
        in_specs=[pl.BlockSpec((step, rows, span), lambda i: (i, 0, 0)) for span in spans],
        out_specs=pl.BlockSpec((rows, step * own), lambda i: (0, i)),
        out_shape=jax.ShapeDtypeStruct((rows, parts * own), jnp.bfloat16),
        compiler_params=pltpu.CompilerParams(vmem_limit_bytes=20 * MIB),
        cost_estimate=pl.CostEstimate(flops=0, bytes_accessed=4 * rows * parts * own, transcendentals=0),
        name="unpack",
    )(*pieces)


def swap(blocks):
    return lax.all_to_all(blocks, "seq", 0, 0, tiled=True)


def ways(parts):
    return [(dx, dy) for dx in range(parts // 2) for dy in range(2)]


def neighbour(index, way, sign, parts):
    x = lax.rem(index // 2 + sign * way[0] + parts // 2, parts // 2)
    y = lax.rem(index % 2 + way[1], 2)
    return 2 * x + y


class Sender:
    def __init__(self, parts):
        self.parts = parts
        self.done = []

    def send(self, piece, way, after=None):
        pairs = []
        for index in range(self.parts):
            x, y = (index // 2 + way[0]) % (self.parts // 2), (index % 2 + way[1]) % 2
            pairs.append((index, 2 * x + y))
        before = self.done[-WINDOW:][:1] if len(self.done) >= WINDOW else []
        if after is not None:
            before = before + [after]
        if before:
            piece, _ = lax.optimization_barrier((piece, before))
        self.done.append(lax.ppermute(piece, "seq", pairs))
        return self.done[-1]

    def send_some(self, pieces, arrived, chosen, after=None):
        all_ways = ways(self.parts)
        for way in chosen:
            arrived[all_ways.index(way)] = self.send(pieces[all_ways.index(way)], way, after)


def shards(query_rows, key_rows, value_rows, query_gain, key_gain, tile_lists, tile_counts):
    parts = lax.axis_size("seq")
    _, rows, width = query_rows.shape
    length = rows * parts
    blocks = length // BLK
    me = lax.axis_index("seq")
    targets = jnp.stack([neighbour(me, way, 1, parts) for way in ways(parts)]).astype(jnp.int32)
    sources = jnp.stack([neighbour(me, way, -1, parts) for way in ways(parts)]).astype(jnp.int32)

    sender = Sender(parts)
    args = (query_rows[0], key_rows[0], value_rows[0], query_gain[None], key_gain[None])
    lead = pack_pieces(*args, targets, 0, SPLIT)
    lead_in = list(lead)
    sender.send_some(lead, lead_in, ORDER)
    args, tile_lists, tile_counts, _ = lax.optimization_barrier((args, tile_lists, tile_counts, sender.done[1]))
    rest = pack_heads(*args, parts, SPLIT, tile_lists.shape[1])
    rest, _ = lax.optimization_barrier((rest, sender.done[EARLY - 1]))
    rest = swap(rest)

    clip_index = lax.axis_index("clip")
    lists = lax.dynamic_index_in_dim(tile_lists, clip_index, 0, keepdims=False)
    counts = lax.dynamic_index_in_dim(tile_counts, clip_index, 0, keepdims=False)
    live = jnp.arange(blocks, dtype=jnp.int32) < counts[..., None]
    named = lists[..., None] == (jnp.arange(length, dtype=jnp.int32) // BLK)
    bias = jnp.where(jnp.any(named & live[..., None], axis=2), 0.0, -1e30).astype(jnp.float32)

    mixed = attend_pieces(lead_in, bias, sources, 0)
    mixed = attend_blocks(rest.reshape(length, rest.shape[2]), bias, SPLIT, mixed)
    home = swap(mixed.reshape(parts, rows, mixed.shape[1]))
    return unpack_heads([home])[None]


def solution(mesh):
    in_specs = (
        P("clip", "seq", None),
        P("clip", "seq", None),
        P("clip", "seq", None),
        P(),
        P(),
        P(None, "seq", None, None),
        P(None, "seq", None),
    )
    out_specs = P("clip", "seq", None)
    return jax.shard_map(shards, mesh=mesh, in_specs=in_specs, out_specs=out_specs, check_vma=False)
```

```python
import math

import jax
import jax.numpy as jnp
from jax import lax
from jax.experimental import pallas as pl
from jax.experimental.pallas import tpu as pltpu
from jax.sharding import PartitionSpec as P

HD = 128
BLK = 128
EPSILON = 1e-06
SPLIT = 3
ORDER = ((1, 0), (3, 1), (3, 0), (1, 1), (0, 1), (2, 0), (2, 1))
WINDOW = 5
EARLY = 4
MIB = 1 << 20


def pack_heads(query_rows, key_rows, value_rows, query_gain, key_gain, parts, first, last):
    rows, width = query_rows.shape
    own = width // parts
    span = (last - first) * HD
    step = rows // 2

    def kernel(q_ref, k_ref, v_ref, qg_ref, kg_ref, out_ref):
        def inverse(ref):
            values = ref[...].astype(jnp.float32)
            return lax.rsqrt(jnp.mean(values * values, axis=-1, keepdims=True) + EPSILON)

        def scaled(ref, factor, gain_ref, cols):
            return (ref[:, cols].astype(jnp.float32) * factor * gain_ref[:, cols]).astype(jnp.bfloat16)

        q_factor = inverse(q_ref)
        k_factor = inverse(k_ref)
        for part in range(parts):
            cols = slice(part * own + first * HD, part * own + last * HD)
            out_ref[part, :, :span] = scaled(q_ref, q_factor, qg_ref, cols)
            out_ref[part, :, span : 2 * span] = scaled(k_ref, k_factor, kg_ref, cols)
            out_ref[part, :, 2 * span :] = v_ref[:, cols]

    row_spec = pl.BlockSpec((step, width), lambda i: (i, 0))
    gain_spec = pl.BlockSpec((1, width), lambda i: (0, 0))
    return pl.pallas_call(
        kernel,
        grid=(rows // step,),
        in_specs=[row_spec, row_spec, row_spec, gain_spec, gain_spec],
        out_specs=pl.BlockSpec((parts, step, 3 * span), lambda i: (0, i, 0)),
        out_shape=jax.ShapeDtypeStruct((parts, rows, 3 * span), jnp.bfloat16),
        compiler_params=pltpu.CompilerParams(vmem_limit_bytes=60 * MIB),
        cost_estimate=pl.CostEstimate(flops=12 * rows * width, bytes_accessed=12 * rows * width, transcendentals=0),
        name=f"pack_{first}",
    )(query_rows, key_rows, value_rows, query_gain, key_gain)


def pack_pieces(query_rows, key_rows, value_rows, query_gain, key_gain, targets, first, last):
    rows, width = query_rows.shape
    parts = targets.shape[0]
    own = width // parts
    span = (last - first) * HD
    step = rows // 2

    def kernel(target_ref, q_ref, k_ref, v_ref, qg_ref, kg_ref, *out_refs):
        def inverse(ref):
            values = ref[...].astype(jnp.float32)
            return lax.rsqrt(jnp.mean(values * values, axis=-1, keepdims=True) + EPSILON)

        def scaled(ref, factor, gain_ref, cols):
            return (ref[:, cols].astype(jnp.float32) * factor * gain_ref[:, cols]).astype(jnp.bfloat16)

        q_factor = inverse(q_ref)
        k_factor = inverse(k_ref)
        for o, out_ref in enumerate(out_refs):
            cols = pl.ds(pl.multiple_of(target_ref[o] * own + first * HD, HD), span)
            out_ref[:, :span] = scaled(q_ref, q_factor, qg_ref, cols)
            out_ref[:, span : 2 * span] = scaled(k_ref, k_factor, kg_ref, cols)
            out_ref[:, 2 * span :] = v_ref[:, cols]

    row_spec = pl.BlockSpec((step, width), lambda i, t: (i, 0))
    gain_spec = pl.BlockSpec((1, width), lambda i, t: (0, 0))
    return pl.pallas_call(
        kernel,
        grid_spec=pltpu.PrefetchScalarGridSpec(
            num_scalar_prefetch=1,
            grid=(rows // step,),
            in_specs=[row_spec, row_spec, row_spec, gain_spec, gain_spec],
            out_specs=[pl.BlockSpec((step, 3 * span), lambda i, t: (i, 0))] * parts,
        ),
        out_shape=[jax.ShapeDtypeStruct((rows, 3 * span), jnp.bfloat16)] * parts,
        compiler_params=pltpu.CompilerParams(vmem_limit_bytes=60 * MIB),
        cost_estimate=pl.CostEstimate(flops=12 * rows * width, bytes_accessed=12 * rows * width, transcendentals=0),
        name=f"pack_pieces_{first}",
    )(targets, query_rows, key_rows, value_rows, query_gain, key_gain)


def one_head(q_ref, k_ref, v_ref, bias_ref, out_ref):
    length = q_ref.shape[0]
    factor = math.log2(math.e) / math.sqrt(HD)

    def scored(i):
        raw = lax.dot_general(
            q_ref[i * BLK : (i + 1) * BLK, :],
            k_ref[...],
            (((1,), (1,)), ((), ())),
            preferred_element_type=jnp.float32,
        )
        return raw + bias_ref[i : i + 1, :]

    def finish(i, scores):
        top = jnp.max(scores, axis=-1, keepdims=True)
        weights = jnp.exp2((scores - top) * factor)
        total = jnp.sum(weights, axis=-1, keepdims=True)
        mixed = jnp.dot(weights.astype(jnp.bfloat16), v_ref[...], preferred_element_type=jnp.float32)
        out_ref[i * BLK : (i + 1) * BLK, :] = (mixed / total).astype(jnp.bfloat16)

    scores = scored(0)
    for i in range(length // BLK):
        ahead = scored(i + 1) if (i + 1) * BLK < length else None
        finish(i, scores)
        scores = ahead


def attend_pieces(pieces, bias, sources, first):
    parts = len(pieces)
    rows, width = pieces[0].shape
    heads = width // (3 * HD)
    all_heads, blocks, length = bias.shape

    def kernel(source_ref, bias_ref, *refs):
        in_refs = refs[:parts]
        out_ref, held, done, in_sems, out_sems = refs[parts:]

        def arrival(o, h, j):
            at = pl.multiple_of(source_ref[o] * rows, 64)
            cols = pl.ds((j * heads + h) * HD, HD)
            return pltpu.make_async_copy(in_refs[o].at[:, cols], held.at[pl.ds(at, rows), cols], in_sems.at[h, j, o])

        def departure(h):
            return pltpu.make_async_copy(
                done.at[:, pl.ds(h * HD, HD)], out_ref.at[:, pl.ds((first + h) * HD, HD)], out_sems.at[h]
            )

        for h in range(heads):
            for j in range(3):
                for o in range(parts):
                    arrival(o, h, j).start()
        for h in range(heads):
            for j in range(3):
                for o in range(parts):
                    arrival(o, h, j).wait()
            q, k, v = (held.at[:, (j * heads + h) * HD : (j * heads + h + 1) * HD] for j in range(3))
            one_head(q, k, v, bias_ref.at[first + h], done.at[:, h * HD : (h + 1) * HD])
            departure(h).start()
        for h in range(heads):
            departure(h).wait()

    anywhere = pl.BlockSpec(memory_space=pl.ANY)
    return pl.pallas_call(
        kernel,
        in_specs=[pl.BlockSpec(memory_space=pltpu.SMEM), pl.BlockSpec(memory_space=pltpu.VMEM)]
        + [anywhere] * parts,
        out_specs=anywhere,
        out_shape=jax.ShapeDtypeStruct((length, all_heads * HD), jnp.bfloat16),
        scratch_shapes=[
            pltpu.VMEM((length, width), jnp.bfloat16),
            pltpu.VMEM((length, heads * HD), jnp.bfloat16),
            pltpu.SemaphoreType.DMA((heads, 3, parts)),
            pltpu.SemaphoreType.DMA((heads,)),
        ],
        compiler_params=pltpu.CompilerParams(vmem_limit_bytes=60 * MIB),
        cost_estimate=pl.CostEstimate(
            flops=12 * heads * length * length * HD,
            bytes_accessed=8 * heads * length * HD,
            transcendentals=3 * heads * length * length,
        ),
        name=f"attend_{heads}",
    )(sources, bias, *pieces)


def attend_blocks(packed, bias, first, mixed):
    length, width = packed.shape
    heads = width // (3 * HD)
    blocks = bias.shape[1]

    def kernel(q_ref, k_ref, v_ref, bias_ref, mixed_ref, out_ref):
        one_head(q_ref, k_ref, v_ref, bias_ref.at[0], out_ref)

    return pl.pallas_call(
        kernel,
        grid=(heads,),
        in_specs=[
            pl.BlockSpec((length, HD), lambda h: (0, h)),
            pl.BlockSpec((length, HD), lambda h: (0, heads + h)),
            pl.BlockSpec((length, HD), lambda h: (0, 2 * heads + h)),
            pl.BlockSpec((1, blocks, length), lambda h: (first + h, 0, 0)),
            pl.BlockSpec(memory_space=pl.ANY),
        ],
        out_specs=pl.BlockSpec((length, HD), lambda h: (0, first + h)),
        out_shape=jax.ShapeDtypeStruct(mixed.shape, mixed.dtype),
        input_output_aliases={4: 0},
        compiler_params=pltpu.CompilerParams(vmem_limit_bytes=60 * MIB),
        cost_estimate=pl.CostEstimate(
            flops=4 * heads * length * length * HD,
            bytes_accessed=8 * heads * length * HD,
            transcendentals=heads * length * length,
        ),
        name="attend_blocks",
    )(packed, packed, packed, bias, mixed)


def unpack_heads(pieces):
    parts, rows, _ = pieces[0].shape
    spans = [piece.shape[2] for piece in pieces]
    own = sum(spans)
    step = parts // 2

    def kernel(*refs):
        out_ref = refs[-1]
        at = 0
        for i in range(step):
            for ref, span in zip(refs[:-1], spans):
                out_ref[:, at : at + span] = ref[i]
                at += span

    return pl.pallas_call(
        kernel,
        grid=(parts // step,),
        in_specs=[pl.BlockSpec((step, rows, span), lambda i: (i, 0, 0)) for span in spans],
        out_specs=pl.BlockSpec((rows, step * own), lambda i: (0, i)),
        out_shape=jax.ShapeDtypeStruct((rows, parts * own), jnp.bfloat16),
        compiler_params=pltpu.CompilerParams(vmem_limit_bytes=20 * MIB),
        cost_estimate=pl.CostEstimate(flops=0, bytes_accessed=4 * rows * parts * own, transcendentals=0),
        name="unpack",
    )(*pieces)


def swap(blocks):
    return lax.all_to_all(blocks, "seq", 0, 0, tiled=True)


def ways(parts):
    return [(dx, dy) for dx in range(parts // 2) for dy in range(2)]


def neighbour(index, way, sign, parts):
    x = lax.rem(index // 2 + sign * way[0] + parts // 2, parts // 2)
    y = lax.rem(index % 2 + way[1], 2)
    return 2 * x + y


class Sender:
    def __init__(self, parts):
        self.parts = parts
        self.done = []

    def send(self, piece, way, after=None):
        pairs = []
        for index in range(self.parts):
            x, y = (index // 2 + way[0]) % (self.parts // 2), (index % 2 + way[1]) % 2
            pairs.append((index, 2 * x + y))
        before = self.done[-WINDOW:][:1] if len(self.done) >= WINDOW else []
        if after is not None:
            before = before + [after]
        if before:
            piece, _ = lax.optimization_barrier((piece, before))
        self.done.append(lax.ppermute(piece, "seq", pairs))
        return self.done[-1]

    def send_some(self, pieces, arrived, chosen, after=None):
        all_ways = ways(self.parts)
        for way in chosen:
            arrived[all_ways.index(way)] = self.send(pieces[all_ways.index(way)], way, after)


def shards(query_rows, key_rows, value_rows, query_gain, key_gain, tile_lists, tile_counts):
    parts = lax.axis_size("seq")
    _, rows, width = query_rows.shape
    length = rows * parts
    blocks = length // BLK
    me = lax.axis_index("seq")
    targets = jnp.stack([neighbour(me, way, 1, parts) for way in ways(parts)]).astype(jnp.int32)
    sources = jnp.stack([neighbour(me, way, -1, parts) for way in ways(parts)]).astype(jnp.int32)

    sender = Sender(parts)
    args = (query_rows[0], key_rows[0], value_rows[0], query_gain[None], key_gain[None])
    lead = pack_pieces(*args, targets, 0, SPLIT)
    lead_in = list(lead)
    sender.send_some(lead, lead_in, ORDER)
    args, tile_lists, tile_counts, _ = lax.optimization_barrier((args, tile_lists, tile_counts, sender.done[1]))
    rest = pack_heads(*args, parts, SPLIT, tile_lists.shape[1])
    rest, _ = lax.optimization_barrier((rest, sender.done[EARLY - 1]))
    rest = swap(rest)

    clip_index = lax.axis_index("clip")
    lists = lax.dynamic_index_in_dim(tile_lists, clip_index, 0, keepdims=False)
    counts = lax.dynamic_index_in_dim(tile_counts, clip_index, 0, keepdims=False)
    live = jnp.arange(blocks, dtype=jnp.int32) < counts[..., None]
    named = lists[..., None] == (jnp.arange(length, dtype=jnp.int32) // BLK)
    bias = jnp.where(jnp.any(named & live[..., None], axis=2), 0.0, -1e30).astype(jnp.float32)

    mixed = attend_pieces(lead_in, bias, sources, 0)
    mixed = attend_blocks(rest.reshape(length, rest.shape[2]), bias, SPLIT, mixed)
    home = swap(mixed.reshape(parts, rows, mixed.shape[1]))
    return unpack_heads([home])[None]


def solution(mesh):
    in_specs = (
        P("clip", "seq", None),
        P("clip", "seq", None),
        P("clip", "seq", None),
        P(),
        P(),
        P(None, "seq", None, None),
        P(None, "seq", None),
    )
    out_specs = P("clip", "seq", None)
    return jax.shard_map(shards, mesh=mesh, in_specs=in_specs, out_specs=out_specs, check_vma=False)
```

```python
import math

import jax
import jax.numpy as jnp
from jax import lax
from jax.experimental import pallas as pl
from jax.experimental.pallas import tpu as pltpu
from jax.sharding import PartitionSpec as P

HD = 128
BLK = 128
EPSILON = 1e-06
SPLIT = 3
ORDER = ((1, 0), (3, 1), (3, 0), (1, 1), (0, 1), (2, 0), (2, 1))
WINDOW = 5
EARLY = 4
MIB = 1 << 20


def pack_heads(query_rows, key_rows, value_rows, query_gain, key_gain, parts, first, last):
    rows, width = query_rows.shape
    own = width // parts
    span = (last - first) * HD
    step = rows // 2

    def kernel(q_ref, k_ref, v_ref, qg_ref, kg_ref, out_ref):
        def inverse(ref):
            values = ref[...].astype(jnp.float32)
            return lax.rsqrt(jnp.mean(values * values, axis=-1, keepdims=True) + EPSILON)

        def scaled(ref, factor, gain_ref, cols):
            return (ref[:, cols].astype(jnp.float32) * factor * gain_ref[:, cols]).astype(jnp.bfloat16)

        q_factor = inverse(q_ref)
        k_factor = inverse(k_ref)
        for part in range(parts):
            cols = slice(part * own + first * HD, part * own + last * HD)
            out_ref[part, :, :span] = scaled(q_ref, q_factor, qg_ref, cols)
            out_ref[part, :, span : 2 * span] = scaled(k_ref, k_factor, kg_ref, cols)
            out_ref[part, :, 2 * span :] = v_ref[:, cols]

    row_spec = pl.BlockSpec((step, width), lambda i: (i, 0))
    gain_spec = pl.BlockSpec((1, width), lambda i: (0, 0))
    return pl.pallas_call(
        kernel,
        grid=(rows // step,),
        in_specs=[row_spec, row_spec, row_spec, gain_spec, gain_spec],
        out_specs=pl.BlockSpec((parts, step, 3 * span), lambda i: (0, i, 0)),
        out_shape=jax.ShapeDtypeStruct((parts, rows, 3 * span), jnp.bfloat16),
        compiler_params=pltpu.CompilerParams(vmem_limit_bytes=60 * MIB),
        cost_estimate=pl.CostEstimate(flops=12 * rows * width, bytes_accessed=12 * rows * width, transcendentals=0),
        name=f"pack_{first}",
    )(query_rows, key_rows, value_rows, query_gain, key_gain)


def pack_pieces(query_rows, key_rows, value_rows, query_gain, key_gain, targets, first, last):
    rows, width = query_rows.shape
    parts = targets.shape[0]
    own = width // parts
    span = (last - first) * HD
    step = rows // 2

    def kernel(target_ref, q_ref, k_ref, v_ref, qg_ref, kg_ref, *out_refs):
        def inverse(ref):
            values = ref[...].astype(jnp.float32)
            return lax.rsqrt(jnp.mean(values * values, axis=-1, keepdims=True) + EPSILON)

        def scaled(ref, factor, gain_ref, cols):
            return (ref[:, cols].astype(jnp.float32) * factor * gain_ref[:, cols]).astype(jnp.bfloat16)

        q_factor = inverse(q_ref)
        k_factor = inverse(k_ref)
        for o, out_ref in enumerate(out_refs):
            cols = pl.ds(pl.multiple_of(target_ref[o] * own + first * HD, HD), span)
            out_ref[:, :span] = scaled(q_ref, q_factor, qg_ref, cols)
            out_ref[:, span : 2 * span] = scaled(k_ref, k_factor, kg_ref, cols)
            out_ref[:, 2 * span :] = v_ref[:, cols]

    row_spec = pl.BlockSpec((step, width), lambda i, t: (i, 0))
    gain_spec = pl.BlockSpec((1, width), lambda i, t: (0, 0))
    return pl.pallas_call(
        kernel,
        grid_spec=pltpu.PrefetchScalarGridSpec(
            num_scalar_prefetch=1,
            grid=(rows // step,),
            in_specs=[row_spec, row_spec, row_spec, gain_spec, gain_spec],
            out_specs=[pl.BlockSpec((step, 3 * span), lambda i, t: (i, 0))] * parts,
        ),
        out_shape=[jax.ShapeDtypeStruct((rows, 3 * span), jnp.bfloat16)] * parts,
        compiler_params=pltpu.CompilerParams(vmem_limit_bytes=60 * MIB),
        cost_estimate=pl.CostEstimate(flops=12 * rows * width, bytes_accessed=12 * rows * width, transcendentals=0),
        name=f"pack_pieces_{first}",
    )(targets, query_rows, key_rows, value_rows, query_gain, key_gain)


def one_head(q_ref, k_ref, v_ref, bias_ref, out_ref):
    length = q_ref.shape[0]
    factor = math.log2(math.e) / math.sqrt(HD)

    def scored(i):
        raw = lax.dot_general(
            q_ref[i * BLK : (i + 1) * BLK, :],
            k_ref[...],
            (((1,), (1,)), ((), ())),
            preferred_element_type=jnp.float32,
        )
        return raw + bias_ref[i : i + 1, :]

    def finish(i, scores):
        top = jnp.max(scores, axis=-1, keepdims=True)
        weights = jnp.exp2((scores - top) * factor)
        total = jnp.sum(weights, axis=-1, keepdims=True)
        mixed = jnp.dot(weights.astype(jnp.bfloat16), v_ref[...], preferred_element_type=jnp.float32)
        out_ref[i * BLK : (i + 1) * BLK, :] = (mixed / total).astype(jnp.bfloat16)

    scores = scored(0)
    for i in range(length // BLK):
        ahead = scored(i + 1) if (i + 1) * BLK < length else None
        finish(i, scores)
        scores = ahead


def attend_pieces(pieces, bias, sources, first):
    parts = len(pieces)
    rows, width = pieces[0].shape
    heads = width // (3 * HD)
    all_heads, blocks, length = bias.shape

    def kernel(source_ref, bias_ref, *refs):
        in_refs = refs[:parts]
        out_ref, held, done, in_sems, out_sems = refs[parts:]

        def arrival(o, h, j):
            at = pl.multiple_of(source_ref[o] * rows, 64)
            cols = pl.ds((j * heads + h) * HD, HD)
            return pltpu.make_async_copy(in_refs[o].at[:, cols], held.at[pl.ds(at, rows), cols], in_sems.at[h, j, o])

        def departure(h):
            return pltpu.make_async_copy(
                done.at[:, pl.ds(h * HD, HD)], out_ref.at[:, pl.ds((first + h) * HD, HD)], out_sems.at[h]
            )

        for h in range(heads):
            for j in range(3):
                for o in range(parts):
                    arrival(o, h, j).start()
        for h in range(heads):
            for j in range(3):
                for o in range(parts):
                    arrival(o, h, j).wait()
            q, k, v = (held.at[:, (j * heads + h) * HD : (j * heads + h + 1) * HD] for j in range(3))
            one_head(q, k, v, bias_ref.at[first + h], done.at[:, h * HD : (h + 1) * HD])
            departure(h).start()
        for h in range(heads):
            departure(h).wait()

    anywhere = pl.BlockSpec(memory_space=pl.ANY)
    return pl.pallas_call(
        kernel,
        in_specs=[pl.BlockSpec(memory_space=pltpu.SMEM), pl.BlockSpec(memory_space=pltpu.VMEM)]
        + [anywhere] * parts,
        out_specs=anywhere,
        out_shape=jax.ShapeDtypeStruct((length, all_heads * HD), jnp.bfloat16),
        scratch_shapes=[
            pltpu.VMEM((length, width), jnp.bfloat16),
            pltpu.VMEM((length, heads * HD), jnp.bfloat16),
            pltpu.SemaphoreType.DMA((heads, 3, parts)),
            pltpu.SemaphoreType.DMA((heads,)),
        ],
        compiler_params=pltpu.CompilerParams(vmem_limit_bytes=60 * MIB),
        cost_estimate=pl.CostEstimate(
            flops=12 * heads * length * length * HD,
            bytes_accessed=8 * heads * length * HD,
            transcendentals=3 * heads * length * length,
        ),
        name=f"attend_{heads}",
    )(sources, bias, *pieces)


def attend_blocks(packed, bias, first, mixed):
    length, width = packed.shape
    heads = width // (3 * HD)
    blocks = bias.shape[1]

    def kernel(q_ref, k_ref, v_ref, bias_ref, mixed_ref, out_ref):
        one_head(q_ref, k_ref, v_ref, bias_ref.at[0], out_ref)

    return pl.pallas_call(
        kernel,
        grid=(heads,),
        in_specs=[
            pl.BlockSpec((length, HD), lambda h: (0, h)),
            pl.BlockSpec((length, HD), lambda h: (0, heads + h)),
            pl.BlockSpec((length, HD), lambda h: (0, 2 * heads + h)),
            pl.BlockSpec((1, blocks, length), lambda h: (first + h, 0, 0)),
            pl.BlockSpec(memory_space=pl.ANY),
        ],
        out_specs=pl.BlockSpec((length, HD), lambda h: (0, first + h)),
        out_shape=jax.ShapeDtypeStruct(mixed.shape, mixed.dtype),
        input_output_aliases={4: 0},
        compiler_params=pltpu.CompilerParams(vmem_limit_bytes=28 * MIB),
        cost_estimate=pl.CostEstimate(
            flops=4 * heads * length * length * HD,
            bytes_accessed=8 * heads * length * HD,
            transcendentals=heads * length * length,
        ),
        name="attend_blocks",
    )(packed, packed, packed, bias, mixed)


def unpack_heads(pieces):
    parts, rows, _ = pieces[0].shape
    spans = [piece.shape[2] for piece in pieces]
    own = sum(spans)
    step = parts // 2

    def kernel(*refs):
        out_ref = refs[-1]
        at = 0
        for i in range(step):
            for ref, span in zip(refs[:-1], spans):
                out_ref[:, at : at + span] = ref[i]
                at += span

    return pl.pallas_call(
        kernel,
        grid=(parts // step,),
        in_specs=[pl.BlockSpec((step, rows, span), lambda i: (i, 0, 0)) for span in spans],
        out_specs=pl.BlockSpec((rows, step * own), lambda i: (0, i)),
        out_shape=jax.ShapeDtypeStruct((rows, parts * own), jnp.bfloat16),
        compiler_params=pltpu.CompilerParams(vmem_limit_bytes=20 * MIB),
        cost_estimate=pl.CostEstimate(flops=0, bytes_accessed=4 * rows * parts * own, transcendentals=0),
        name="unpack",
    )(*pieces)


def swap(blocks):
    return lax.all_to_all(blocks, "seq", 0, 0, tiled=True)


def ways(parts):
    return [(dx, dy) for dx in range(parts // 2) for dy in range(2)]


def neighbour(index, way, sign, parts):
    x = lax.rem(index // 2 + sign * way[0] + parts // 2, parts // 2)
    y = lax.rem(index % 2 + way[1], 2)
    return 2 * x + y


class Sender:
    def __init__(self, parts):
        self.parts = parts
        self.done = []

    def send(self, piece, way, after=None):
        pairs = []
        for index in range(self.parts):
            x, y = (index // 2 + way[0]) % (self.parts // 2), (index % 2 + way[1]) % 2
            pairs.append((index, 2 * x + y))
        before = self.done[-WINDOW:][:1] if len(self.done) >= WINDOW else []
        if after is not None:
            before = before + [after]
        if before:
            piece, _ = lax.optimization_barrier((piece, before))
        self.done.append(lax.ppermute(piece, "seq", pairs))
        return self.done[-1]

    def send_some(self, pieces, arrived, chosen, after=None):
        all_ways = ways(self.parts)
        for way in chosen:
            arrived[all_ways.index(way)] = self.send(pieces[all_ways.index(way)], way, after)


def shards(query_rows, key_rows, value_rows, query_gain, key_gain, tile_lists, tile_counts):
    parts = lax.axis_size("seq")
    _, rows, width = query_rows.shape
    length = rows * parts
    blocks = length // BLK
    me = lax.axis_index("seq")
    targets = jnp.stack([neighbour(me, way, 1, parts) for way in ways(parts)]).astype(jnp.int32)
    sources = jnp.stack([neighbour(me, way, -1, parts) for way in ways(parts)]).astype(jnp.int32)

    sender = Sender(parts)
    args = (query_rows[0], key_rows[0], value_rows[0], query_gain[None], key_gain[None])
    lead = pack_pieces(*args, targets, 0, SPLIT)
    lead_in = list(lead)
    sender.send_some(lead, lead_in, ORDER)
    args, tile_lists, tile_counts, _ = lax.optimization_barrier((args, tile_lists, tile_counts, sender.done[1]))
    rest = pack_heads(*args, parts, SPLIT, tile_lists.shape[1])
    rest, _ = lax.optimization_barrier((rest, sender.done[EARLY - 1]))
    rest = swap(rest)

    clip_index = lax.axis_index("clip")
    lists = lax.dynamic_index_in_dim(tile_lists, clip_index, 0, keepdims=False)
    counts = lax.dynamic_index_in_dim(tile_counts, clip_index, 0, keepdims=False)
    live = jnp.arange(blocks, dtype=jnp.int32) < counts[..., None]
    named = lists[..., None] == (jnp.arange(length, dtype=jnp.int32) // BLK)
    bias = jnp.where(jnp.any(named & live[..., None], axis=2), 0.0, -1e30).astype(jnp.float32)

    mixed = attend_pieces(lead_in, bias, sources, 0)
    mixed = attend_blocks(rest.reshape(length, rest.shape[2]), bias, SPLIT, mixed)
    home = swap(mixed.reshape(parts, rows, mixed.shape[1]))
    return unpack_heads([home])[None]


def solution(mesh):
    in_specs = (
        P("clip", "seq", None),
        P("clip", "seq", None),
        P("clip", "seq", None),
        P(),
        P(),
        P(None, "seq", None, None),
        P(None, "seq", None),
    )
    out_specs = P("clip", "seq", None)
    return jax.shard_map(shards, mesh=mesh, in_specs=in_specs, out_specs=out_specs, check_vma=False)
```
